256 devices in a mesh: ex: 64 (over z, y, core), tp: 4 (over x).
Axes of the slice: x: 4, y: 4, z: 8, core: 2. Of those that a mesh axis runs over, the one named last changes fastest.
Arguments:
- residual_in: bfloat16 [12288, 2880], P('ex', 'tp'), may hold values from -40 to 40
- queries: bfloat16 [12288, 2048], P('ex', 'tp'), may hold values from -4 to 4
- keys_values: bfloat16 [12288, 4, 128], P('ex', 'tp'), may hold values from -4 to 4
- sink_logits: float32 [32], P('tp'), may hold values from 1 to 6
- out_proj: bfloat16 [2048, 2880], P('tp'), may hold values from -0.75 to 0.75
- norm_gain: float32 [2880], replicated, may hold values from 0.25 to 1.75
- routes: int32 [12288, 4], P('ex'), may hold values from 0 to 63, all different within a row; in each aligned block of 192 rows (0 to 191, 192 to 383, ...) at most 20 rows name the same one
- route_scores: int32 [12288, 4], P('ex'), may hold values from 1 to 8
- tenants: int32 [12288], P('ex'), may hold values from 0 to 7
- gate_up: bfloat16 [64, 2880, 2, 1536], P('ex', None, None, 'tp'), may hold values from -0.109375 to 0.109375
- adapter_in: bfloat16 [64, 2880, 128], P('ex'), may hold values from -0.109375 to 0.109375
- adapter_out: bfloat16 [64, 128, 2, 1536], P('ex', None, None, 'tp'), may hold values from -1.5 to 1.5
- down_proj: bfloat16 [64, 1536, 2880], P('ex', 'tp'), may hold values from -0.15625 to 0.15625
Outputs:
- residual_out: bfloat16 [12288, 2880], P('ex', 'tp')
- expert_mix: bfloat16 [12288, 2880], P('ex', 'tp')
The draws below stay inside these ranges and needn't reach their ends.
Inputs may be any that keep to these rules, and one draw needn't show every extreme that they name: `routes`: among the 192 rows of one device (aligned blocks), no expert is named by more than 20 rows, and in every draw some expert is named by exactly 20 rows of some block.
All inputs are finite; a program needn't handle non-finite values.
Results may differ from the reference program's by a relative error of at most 0.023.
Values may be sent and summed in bfloat16 or wider, within the bound.
No kernel may reach another device: no remote copies, remote signals or barrier semaphores. Data moves between devices by JAX's collectives and lax.ppermute only.
A program may use at most 128 MiB of HBM per device.

```python
import math
import jax
import jax.numpy as jnp
import numpy as np
from jax import lax

D = 2880
HD = 64
QH = 32
KVH = 4
WINDOW = 128
EXPERTS = 64
TOP = 4
FFE = 1536
TENANTS = 8
RANK = 16
TOK_DEV = 192
TOKENS = 12288
CAP = 20
N_EX = 64
N_TP = 4


def draw_residual_in(key, part):
    key_row, key_col, key_base = jax.random.split(key, 3)
    row_power = jax.random.uniform(key_row, (TOKENS, 1), jnp.float32)
    col_place = jnp.arange(D, dtype=jnp.float32)[None, :] / D
    col_power = 0.5 * col_place + 0.5 * jax.random.uniform(key_col, (1, D), jnp.float32)
    scales = 10.0 ** (row_power + col_power - 1.0)
    base = jnp.clip(jax.random.normal(key_base, (TOKENS, D), jnp.float32), -4.0, 4.0)
    return (base * scales).astype(jnp.bfloat16)


def set_ends(drawn, rng, least, high):
    longest = drawn.shape.index(max(drawn.shape))
    spots = []
    for shift in (0, 1):
        where = [jax.random.randint(jax.random.fold_in(rng, axis), (), 0, length) for axis, length in enumerate(drawn.shape)]
        where[longest] = (where[longest] + shift) % drawn.shape[longest]
        spots.append(tuple(where))
    return drawn.at[spots[0]].set(least).at[spots[1]].set(high)


def block_levels(own_key, extent, cuts, smallest, top_value):
    factor_of = 1.0
    for position, shards_of in cuts:
        steps = jax.random.uniform(jax.random.fold_in(jax.random.fold_in(own_key, 6), position), (shards_of,), jnp.float32, smallest / len(cuts), top_value / len(cuts))
        factor_of = factor_of * jnp.repeat(jnp.exp(steps), extent[position] // shards_of).reshape((-1,) + (1,) * (len(extent) - 1 - position))
    return factor_of


def assign_block(rng, own, number, rows, amount, top, most, lean):
    order = jax.random.permutation(rng, amount)
    heavy_load, ordinary = portions_of(amount, rows * top, most, lean, True), portions_of(amount, rows * top, most, lean, False)
    places = jnp.arange(amount)

    def named(sizes, turn):
        used = int((sizes > 0).sum())
        fixed = max(1, used // 4)
        moved = fixed + (places - fixed + turn * (used - fixed)) % max(1, amount - fixed)
        return jnp.zeros((amount,), jnp.int32).at[order[jnp.where(places < fixed, places, moved)]].set(jnp.asarray(sizes, jnp.int32))

    sizes = jnp.where(number % 4 == 0, named(heavy_load, number // 4), named(ordinary, number - number // 4 - 1))
    mixed = jax.random.permutation(jax.random.fold_in(own, 3), amount)
    source_of, taker = mixed[0:amount // 2 * 2:2], mixed[1:amount // 2 * 2:2]
    room = jnp.minimum(sizes[source_of] - 1, most - sizes[taker]) // 2
    room = jnp.where((source_of == order[0]) | (taker == order[0]) | (sizes[taker] == 0), 0, jnp.maximum(room, 0))
    moved = jax.random.randint(jax.random.fold_in(own, 4), (amount // 2,), 0, 1 << 20) % (room + 1)
    sizes = sizes.at[source_of].add(-moved).at[taker].add(moved)
    labels = jnp.searchsorted(jnp.cumsum(sizes), jnp.arange(rows * top), side="right").astype(jnp.int32)
    table = labels.reshape(top, rows).T
    table = table[jax.random.permutation(jax.random.fold_in(own, 1), rows)]
    turn = jax.random.randint(jax.random.fold_in(own, 2), (rows, 1), 0, top)
    return jnp.take_along_axis(table, (jnp.arange(top)[None, :] + turn) % top, axis=1)


def portions_of(count, total, bound, skew, full):
    weights = [(1 << 20) // math.isqrt(grade ** skew) + 1 for grade in range(1, count + 1)]
    largest = bound if full else min(bound, max(-(-total // count), total * weights[0] // sum(weights)))
    least = 1 if total - largest >= count - 1 else 0
    holding, rest = [largest] + [least] * (count - 1), total - largest - least * (count - 1)
    while rest > 0:
        candidates = [i for i in range(1, count) if holding[i] < largest] or [i for i in range(1, count) if holding[i] < bound]
        whole, remaining = sum([weights[i] for i in candidates]), rest
        for i in candidates:
            addition = min(bound - holding[i], max(1, remaining * weights[i] // whole), rest)
            holding[i] = holding[i] + addition
            rest = rest - addition
    return np.array(holding)


def noise(stream_key, dims, deviation, most, cuts=(), kind=jnp.bfloat16):
    entries = jax.random.normal(stream_key, dims, jnp.float32) * deviation
    if len(cuts) > 0:
        entries = block_levels(stream_key, dims, cuts, -0.22, 0.18) * entries
    return jnp.clip(entries, min=-most, max=most).astype(kind)


def setup_inputs(seed: int = 0) -> dict:
    splits = jax.random.split(jax.random.key(seed), 14)
    residual_in = draw_residual_in(jax.random.fold_in(splits[13], 71), 0)
    queries = noise(splits[1], (TOKENS, QH * HD), 1.0, 4.0, ((0, 64), (1, 4)))
    keys_values = noise(splits[2], (TOKENS, KVH, 2 * HD), 1.0, 4.0, ((0, 64), (1, 4)))
    sink_logits = jnp.clip(1.0 + 5.0 * jax.random.uniform(splits[3], (QH,), jnp.float32) ** block_levels(splits[3], (QH,), ((0, 4),), -0.2, 0.2), 1.0, 6.0)
    out_proj = noise(splits[4], (QH * HD, D), HD ** -0.5, 0.75, ((0, 4),))
    norm_gain = jnp.clip(1.0 + 0.15 * jax.random.normal(splits[5], (D,), jnp.float32), 0.25, 1.75)
    routes_keys = jax.random.split(jax.random.fold_in(splits[6], 1), TOKENS // TOK_DEV)
    routes_turns = jax.random.permutation(jax.random.fold_in(splits[6], 3), TOKENS // TOK_DEV)
    routes = jax.vmap(lambda own, number: assign_block(jax.random.fold_in(splits[6], 2), own, number, TOK_DEV, EXPERTS, TOP, CAP, 2))(routes_keys, routes_turns).reshape((TOKENS, TOP))
    route_scores = set_ends(jax.random.randint(splits[7], (TOKENS, TOP), 1, 9), jax.random.fold_in(splits[7], 1), 1, 8).astype(jnp.int32)
    tenants = set_ends(jax.random.randint(splits[8], (TOKENS,), 0, TENANTS), jax.random.fold_in(splits[8], 1), 0, TENANTS - 1).astype(jnp.int32)
    gate_up = noise(splits[9], (EXPERTS, D, 2, FFE), D ** -0.5, 0.109375, ((0, 64), (3, 4)))
    adapter_in = noise(splits[10], (EXPERTS, D, TENANTS * RANK), D ** -0.5, 0.109375, ((0, 64),))
    adapter_out = noise(splits[11], (EXPERTS, TENANTS * RANK, 2, FFE), RANK ** -0.5, 1.5, ((0, 64), (3, 4)))
    down_proj = noise(splits[12], (EXPERTS, FFE, D), FFE ** -0.5, 0.15625, ((0, 64), (1, 4)))
    return dict(residual_in=residual_in, queries=queries, keys_values=keys_values, sink_logits=sink_logits, out_proj=out_proj, norm_gain=norm_gain, routes=routes, route_scores=route_scores, tenants=tenants, gate_up=gate_up, adapter_in=adapter_in, adapter_out=adapter_out, down_proj=down_proj)


def attend_block(block_id, queries, padded_kv, sink_logits):
    start = block_id * TOK_DEV
    query_rows = lax.dynamic_slice_in_dim(queries, start, TOK_DEV, 0).astype(jnp.float32)
    query_rows = query_rows.reshape(TOK_DEV, KVH, QH // KVH, HD)
    key_rows = lax.dynamic_slice_in_dim(padded_kv, start, TOK_DEV + WINDOW - 1, 0).astype(jnp.float32)
    keys_only = key_rows[:, :, :HD]
    values_only = key_rows[:, :, HD:]
    scores = jnp.einsum('tcgd,jcd->cgtj', query_rows, keys_only) * HD ** (-0.5)
    query_pos = start + jnp.arange(TOK_DEV, dtype=jnp.int32)
    key_pos = start - (WINDOW - 1) + jnp.arange(TOK_DEV + WINDOW - 1, dtype=jnp.int32)
    distance = query_pos[:, None] - key_pos[None, :]
    allowed = (distance >= 0) & (distance < WINDOW) & (key_pos[None, :] >= 0)
    numerators = jnp.where(allowed, jnp.exp(scores), 0.0)
    totals = jnp.exp(sink_logits.reshape(KVH, QH // KVH))[:, :, None] + lax.optimization_barrier(jnp.sum(numerators, axis=-1))
    weights = (numerators / totals[..., None]).astype(jnp.bfloat16)
    result = jnp.einsum('cgtj,jcd->tcgd', weights.astype(jnp.float32), values_only)
    return result.astype(jnp.bfloat16).reshape(TOK_DEV, QH * HD)

def reference(residual_in, queries, keys_values, sink_logits, out_proj, norm_gain, routes, route_scores, tenants, gate_up, adapter_in, adapter_out, down_proj):
    padded_kv = jnp.concatenate([jnp.zeros((WINDOW - 1, KVH, 2 * HD), keys_values.dtype), keys_values], axis=0)
    block_ids = jnp.arange(N_EX, dtype=jnp.int32)
    attended = lax.map(lambda block_id: attend_block(block_id, queries, padded_kv, sink_logits), block_ids)
    attended = attended.reshape(TOKENS, QH * HD)
    projected_heads = jnp.dot(attended, out_proj, preferred_element_type=jnp.float32)
    residual_out = (residual_in.astype(jnp.float32) + projected_heads).astype(jnp.bfloat16)
    widened = lax.optimization_barrier(residual_out).astype(jnp.float32)
    inverse = lax.rsqrt(lax.optimization_barrier(jnp.mean(widened * widened, axis=-1, keepdims=True)) + 1e-05)
    normed = (widened * inverse * norm_gain).astype(jnp.bfloat16)
    pair_count = TOKENS * TOP
    block_routes = routes.reshape(N_EX, TOK_DEV * TOP)
    one_hot = (block_routes[:, :, None] == jnp.arange(EXPERTS, dtype=jnp.int32)[None, None, :]).astype(jnp.int32)
    earlier = jnp.cumsum(one_hot, axis=1) - one_hot
    slot = lax.optimization_barrier(jnp.sum(earlier * one_hot, axis=2))
    source = jnp.arange(N_EX, dtype=jnp.int32)[:, None]
    target = (block_routes * (N_EX * CAP) + source * CAP + slot).reshape(pair_count)
    pair_of = jnp.full((EXPERTS * N_EX * CAP,), pair_count, jnp.int32).at[target].set(jnp.arange(pair_count, dtype=jnp.int32))
    token_of = pair_of // TOP
    score_float = route_scores.astype(jnp.float32)
    route_weight = (score_float / lax.optimization_barrier(jnp.sum(score_float, axis=1, keepdims=True))).reshape(pair_count)
    weight_pad = jnp.concatenate([route_weight, jnp.zeros((1,), jnp.float32)])
    normed_pad = jnp.concatenate([normed, jnp.zeros((1, D), jnp.bfloat16)], axis=0)
    tenant_pad = jnp.concatenate([tenants, jnp.zeros((1,), jnp.int32)])
    slot_tokens = token_of.reshape(EXPERTS, N_EX * CAP)
    slot_weights = weight_pad[pair_of].reshape(EXPERTS, N_EX * CAP)

    def one_expert(carry, packed):
        weight_gu, weight_in, weight_out, weight_down, row_tokens, row_weights = packed
        rows = normed_pad[row_tokens]
        row_tenants = tenant_pad[row_tokens]
        mapped = jnp.dot(rows, weight_gu.reshape(D, 2 * FFE), preferred_element_type=jnp.float32)
        low_rank = jnp.dot(rows, weight_in, preferred_element_type=jnp.float32)
        keep = (jnp.arange(TENANTS * RANK, dtype=jnp.int32) // RANK)[None, :] == row_tenants[:, None]
        low_rank = jnp.where(keep, low_rank, 0.0).astype(jnp.bfloat16)
        mapped = mapped + jnp.dot(low_rank, weight_out.reshape(TENANTS * RANK, 2 * FFE), preferred_element_type=jnp.float32)
        gate_part = mapped[:, :FFE]
        up_part = mapped[:, FFE:]
        activated = (gate_part * jax.nn.sigmoid(1.702 * gate_part) * (up_part + 1.0)).astype(jnp.bfloat16)
        quarters = jnp.einsum('rpf,pfd->prd', activated.astype(jnp.float32).reshape(-1, N_TP, FFE // N_TP), weight_down.astype(jnp.float32).reshape(N_TP, FFE // N_TP, D))
        quarters = lax.optimization_barrier(quarters.astype(jnp.bfloat16)).astype(jnp.float32)
        expert_out = lax.optimization_barrier(jnp.sum(quarters, axis=0))
        return (carry.at[row_tokens].add(expert_out * row_weights[:, None]), None)
    start_mix = jnp.zeros((TOKENS + 1, D), jnp.float32)
    mixed, unused = lax.scan(one_expert, start_mix, (gate_up, adapter_in, adapter_out, down_proj, slot_tokens, slot_weights))
    return (residual_out, mixed[:TOKENS].astype(jnp.bfloat16))
```

```python
import jax
import jax.numpy as jnp
from jax import lax
from jax.sharding import PartitionSpec as P

WINDOW = 128
TOP = 4
RANK = 16
LANES = 128
CHUNKS = (10, 10)


def from_behind(value, axis, steps):
    count = lax.axis_size(axis)
    initial, last = (max(0, -steps), min(count, count - steps))
    return lax.ppermute(value, axis, [(source, source + steps) for source in range(initial, last)])


def rotate(value, axis, steps):
    count = lax.axis_size(axis)
    return lax.ppermute(value, axis, [(source, (source + steps) % count) for source in range(count)])


def ring_gather(value):
    half = value.shape[0] // 2
    behind = rotate(value, "tp", 1)
    ahead = rotate(value, "tp", -1)
    across_top = rotate(behind[:half], "tp", 1)
    across_low = rotate(ahead[half:], "tp", -1)
    return value, behind, ahead, jnp.concatenate([across_top, across_low], axis=0)


def attend(queries, keys_values, sink_logits):
    tok_rows = queries.shape[0]
    heads_here = sink_logits.shape[0]
    kv_here = keys_values.shape[1]
    group_size = heads_here // kv_here
    head_size = keys_values.shape[2] // 2
    rim_rows = WINDOW - 1
    before = from_behind(keys_values[tok_rows - rim_rows :], "ex", 1)
    extended = jnp.concatenate([before, keys_values], axis=0)
    keys_only = extended[:, :, :head_size]
    values_only = extended[:, :, head_size:]
    query_rows = queries.reshape(tok_rows, kv_here, group_size, head_size)
    scores = jnp.einsum(
        "tcgd,jcd->cgtj", query_rows, keys_only, preferred_element_type=jnp.float32
    ) * head_size ** (-0.5)
    start = lax.axis_index("ex") * tok_rows
    query_pos = start + jnp.arange(tok_rows, dtype=jnp.int32)
    key_pos = start - rim_rows + jnp.arange(tok_rows + rim_rows, dtype=jnp.int32)
    distance = query_pos[:, None] - key_pos[None, :]
    allowed = (distance >= 0) & (distance < WINDOW) & (key_pos[None, :] >= 0)
    numerators = jnp.where(allowed, jnp.exp(scores), 0.0)
    totals = jnp.exp(sink_logits.reshape(kv_here, group_size))[:, :, None] + jnp.sum(
        numerators, axis=-1
    )
    weights = (numerators / totals[..., None]).astype(jnp.bfloat16)
    attended = jnp.einsum(
        "cgtj,jcd->tcgd", weights, values_only, preferred_element_type=jnp.float32
    )
    return attended.astype(jnp.bfloat16).reshape(tok_rows, heads_here * head_size)


def shards(
    residual_in,
    queries,
    keys_values,
    sink_logits,
    out_proj,
    norm_gain,
    routes,
    route_scores,
    tenants,
    gate_up,
    adapter_in,
    adapter_out,
    down_proj,
):
    bf16, f32 = jnp.bfloat16, jnp.float32
    tok_rows, cols = residual_in.shape
    width = out_proj.shape[1]
    parts = width // cols
    sources = lax.axis_size("ex")
    hidden_here = gate_up.shape[3]
    rank_cols = adapter_in.shape[2]
    capacity = 5 * tok_rows * TOP // (3 * sources)
    me = lax.axis_index("tp")
    wide = -(-(cols + 3) // LANES) * LANES
    order = [me, (me + 3) % parts, (me + 1) % parts, (me + 2) % parts]

    experts = jnp.arange(sources, dtype=jnp.int32)
    named = routes.T[:, None, :] == experts[None, :, None]
    member = jnp.any(named, axis=0)
    score_of = jnp.sum(jnp.where(named, route_scores.T[:, None, :], 0), axis=0).astype(f32)
    steps = jnp.arange(tok_rows, dtype=jnp.int32)
    earlier = (steps[:, None] < steps[None, :]).astype(bf16)
    place = jnp.dot(member.astype(bf16), earlier, preferred_element_type=f32).astype(jnp.int32)
    place = jnp.where(member, place, -1)
    score_sum = jnp.sum(route_scores.astype(f32), axis=1, keepdims=True)

    both = jnp.concatenate(
        [gate_up[0].reshape(width, 2 * hidden_here), adapter_in[0]], axis=1
    ).reshape(parts, cols, 2 * hidden_here + rank_cols)
    both = jnp.pad(both, ((0, 0), (0, wide - cols), (0, 0)))
    into = [lax.dynamic_index_in_dim(both, at, 0, keepdims=False) for at in order]
    up_map = adapter_out[0].reshape(rank_cols, 2 * hidden_here)
    blocks = down_proj[0].reshape(hidden_here, parts, cols).transpose(1, 0, 2)
    blocks = lax.all_to_all(blocks, "tp", split_axis=0, concat_axis=0, tiled=True)
    blocks = jnp.pad(blocks, ((0, 0), (0, 0), (0, wide - cols)))
    down = [lax.dynamic_index_in_dim(blocks, at, 0, keepdims=False) for at in order]

    attended = attend(queries, keys_values, sink_logits)
    head_terms = jnp.dot(attended, out_proj, preferred_element_type=f32).astype(bf16)
    head_terms = head_terms.reshape(tok_rows, parts, cols).transpose(1, 0, 2)
    head_terms = lax.all_to_all(head_terms, "tp", split_axis=0, concat_axis=0, tiled=True)
    head_share = jnp.sum(head_terms.astype(f32), axis=0)
    residual_out = (residual_in.astype(f32) + head_share).astype(bf16)

    rows = residual_out.astype(f32)
    squares = jnp.sum(rows * rows, axis=1, keepdims=True)
    squares_top = squares.astype(bf16)
    squares_low = (squares - squares_top.astype(f32)).astype(bf16)
    gain_here = lax.dynamic_slice_in_dim(norm_gain, me * cols, cols)
    scaled = (rows * gain_here).astype(bf16)
    message = jnp.concatenate(
        [
            scaled,
            tenants.astype(bf16)[:, None],
            squares_top,
            squares_low,
            jnp.zeros((tok_rows, wide - cols - 3), bf16),
        ],
        axis=1,
    )
    group = wide // LANES
    arrivals, selects, first = [], [], 0
    for slots in CHUNKS:
        here = first + jnp.arange(slots, dtype=jnp.int32)
        first += slots
        select = (place[:, None, :] == here[None, :, None]).reshape(sources * slots, tok_rows)
        selects.append(select)
        sent = jnp.dot(select.astype(bf16), message, preferred_element_type=f32).astype(bf16)
        sent = sent.reshape(sources, slots * group, LANES)
        got = lax.all_to_all(sent, "ex", split_axis=0, concat_axis=0, tiled=True)
        arrivals.append(got.reshape(sources * slots, wide))
    mixed = jnp.zeros((tok_rows, wide), f32)
    for slots, got, select in zip(CHUNKS, arrivals, selects):
        blocks_here = ring_gather(got)
        mapped = sum(
            jnp.dot(x, w, preferred_element_type=f32) for x, w in zip(blocks_here, into)
        )
        square = sum(
            x[:, cols + 1].astype(f32) + x[:, cols + 2].astype(f32) for x in blocks_here
        )
        inverse = lax.rsqrt(square / width + 1e-05)[:, None]
        mapped = mapped * inverse
        tenant = got[:, cols].astype(jnp.int32)
        low_rank = mapped[:, 2 * hidden_here :]
        keep = (jnp.arange(rank_cols, dtype=jnp.int32) // RANK)[None, :] == tenant[:, None]
        low_rank = jnp.where(keep, low_rank, 0.0).astype(bf16)
        mapped = mapped[:, : 2 * hidden_here] + jnp.dot(
            low_rank, up_map, preferred_element_type=f32
        )
        gate_part = mapped[:, :hidden_here]
        up_part = mapped[:, hidden_here:]
        activated = (gate_part * jax.nn.sigmoid(1.702 * gate_part) * (up_part + 1.0)).astype(bf16)
        hidden = ring_gather(activated)
        out = sum(jnp.dot(x, w, preferred_element_type=f32) for x, w in zip(hidden, down))
        out = out.astype(bf16).reshape(sources, slots * group, LANES)
        back = lax.all_to_all(out, "ex", split_axis=0, concat_axis=0, tiled=True)
        back = back.reshape(sources * slots, wide)
        scores_here = jnp.broadcast_to(score_of[:, None, :], (sources, slots, tok_rows))
        take = jnp.where(select, scores_here.reshape(sources * slots, tok_rows), 0.0)
        mixed = mixed + lax.dot_general(
            take.astype(bf16), back, (((0,), (0,)), ((), ())), preferred_element_type=f32
        )
    expert_mix = (mixed[:, :cols] / score_sum).astype(bf16)
    return (residual_out, expert_mix)


def solution(mesh):
    in_specs = (
        P("ex", "tp"),
        P("ex", "tp"),
        P("ex", "tp", None),
        P("tp"),
        P("tp", None),
        P(),
        P("ex", None),
        P("ex", None),
        P("ex"),
        P("ex", None, None, "tp"),
        P("ex", None, None),
        P("ex", None, None, "tp"),
        P("ex", "tp", None),
    )
    out_specs = (P("ex", "tp"), P("ex", "tp"))
    return jax.shard_map(shards, mesh=mesh, in_specs=in_specs, out_specs=out_specs, check_vma=False)
```

```python
import functools

import jax
import jax.numpy as jnp
from jax import lax
from jax.experimental import pallas as pl
from jax.experimental.pallas import tpu as pltpu
from jax.sharding import PartitionSpec as P

WINDOW = 128
TOP = 4
RANK = 16
LANES = 128
CHUNKS = (8, 8, 4)
VMEM_LIMIT = 48 * 1024 * 1024
BF16, F32 = jnp.bfloat16, jnp.float32
NT = (((1,), (1,)), ((), ()))


def params():
    return pltpu.CompilerParams(vmem_limit_bytes=VMEM_LIMIT)


def whole(shape):
    return pl.BlockSpec(shape, lambda *_: (0,) * len(shape))


def cost(flops, moved):
    return pl.CostEstimate(flops=flops, bytes_accessed=moved, transcendentals=0)


def together(*values):
    return lax.optimization_barrier(values)


def from_behind(value, axis, steps):
    count = lax.axis_size(axis)
    initial, last = (max(0, -steps), min(count, count - steps))
    return lax.ppermute(value, axis, [(source, source + steps) for source in range(initial, last)])


def rotate(value, axis, steps):
    count = lax.axis_size(axis)
    return lax.ppermute(value, axis, [(source, (source + steps) % count) for source in range(count)])


def ring_gather(value):
    half = value.shape[0] // 2
    behind = rotate(value, "tp", 1)
    ahead = rotate(value, "tp", -1)
    return value, behind, ahead, rotate(behind[:half], "tp", 1), rotate(ahead[half:], "tp", -1)


def attend_kernel(heads, head_size, first_ref, q_ref, before_ref, kv_ref, sink_ref, proj_ref, out_ref):
    rows = q_ref.shape[0]
    rim = before_ref.shape[0]
    near = jnp.concatenate([before_ref[...], kv_ref[...]], axis=0)
    keys_only = near[:, :head_size]
    values_only = near[:, head_size:]
    at = lax.broadcasted_iota(jnp.int32, (rows, rim + rows), 0)
    key_at = lax.broadcasted_iota(jnp.int32, (rows, rim + rows), 1)
    distance = at + rim - key_at
    allowed = (distance >= 0) & (distance < WINDOW) & (key_at + first_ref[0] >= rim)
    pieces = []
    for head in range(heads):
        query = q_ref[:, head * head_size : (head + 1) * head_size]
        scores = lax.dot_general(query, keys_only, NT, preferred_element_type=F32)
        scores = scores * head_size ** (-0.5)
        numerators = jnp.where(allowed, jnp.exp(scores), 0.0)
        total = jnp.exp(sink_ref[:, head : head + 1]) + jnp.sum(numerators, axis=1, keepdims=True)
        weights = (numerators / total).astype(BF16)
        pieces.append(jnp.dot(weights, values_only, preferred_element_type=F32).astype(BF16))
    attended = jnp.concatenate(pieces, axis=1)
    for part in range(out_ref.shape[0]):
        out_ref[part] = lax.dot_general(
            attended, proj_ref[part], NT, preferred_element_type=F32
        ).astype(BF16)


def attend(queries, keys_values, sink_logits, proj, parts, cols):
    rows = queries.shape[0]
    heads = sink_logits.shape[0]
    head_size = keys_values.shape[2] // 2
    own = keys_values.reshape(rows, 2 * head_size)
    before = from_behind(own[rows - WINDOW :], "ex", 1)
    first = (lax.axis_index("ex") * rows).reshape(1)
    return pl.pallas_call(
        functools.partial(attend_kernel, heads, head_size),
        out_shape=jax.ShapeDtypeStruct((parts, rows, cols), BF16),
        in_specs=[pl.BlockSpec(memory_space=pltpu.SMEM)]
        + [pl.BlockSpec(memory_space=pltpu.VMEM)] * 5,
        out_specs=pl.BlockSpec(memory_space=pltpu.VMEM),
        compiler_params=params(),
        cost_estimate=cost(700_000_000, 5_000_000),
    )(first, queries, before, own, sink_logits.reshape(1, heads), proj)


def send_kernel(
    cols, res_ref, t0, t1, t2, t3, gain_ref, tenant_ref, select_ref, out_ref, message_ref, sent_ref
):
    share = t0[...].astype(F32) + t1[...].astype(F32) + t2[...].astype(F32) + t3[...].astype(F32)
    residual = (res_ref[...].astype(F32) + share).astype(BF16)
    out_ref[...] = residual
    rows = residual.astype(F32)
    squares = jnp.sum(rows * rows, axis=1, keepdims=True)
    top = squares.astype(BF16).astype(F32)
    low = squares - top
    wide = message_ref.shape[1]
    lane = lax.broadcasted_iota(jnp.int32, (rows.shape[0], wide - cols), 1)
    extra = jnp.where(
        lane == 0, tenant_ref[...], jnp.where(lane == 1, top, jnp.where(lane == 2, low, 0.0))
    )
    message = jnp.concatenate([rows * gain_ref[...], extra], axis=1).astype(BF16)
    message_ref[...] = message
    sent_ref[...] = jnp.dot(select_ref[...], message, preferred_element_type=F32).astype(BF16)


def gather_kernel(select_ref, message_ref, sent_ref):
    sent_ref[...] = jnp.dot(
        select_ref[...], message_ref[...], preferred_element_type=F32
    ).astype(BF16)


def gather_rows(select, message):
    return pl.pallas_call(
        gather_kernel,
        out_shape=jax.ShapeDtypeStruct((select.shape[0], message.shape[1]), BF16),
        compiler_params=params(),
        cost_estimate=cost(2 * select.size * message.shape[1], 2_000_000),
    )(select, message)


def prepare_kernel(order_ref, gate_up_ref, in_ref, out_ref):
    cols = in_ref.shape[1]
    hidden = gate_up_ref.shape[3]
    both = gate_up_ref[0].astype(F32)
    out_ref[0, :cols, :hidden] = both[:, 0, :].astype(BF16)
    out_ref[0, :cols, hidden : 2 * hidden] = both[:, 1, :].astype(BF16)
    out_ref[0, :cols, 2 * hidden :] = in_ref[0]
    out_ref[0, cols:, :] = jnp.zeros_like(out_ref[0, cols:, :])


def prepare(order, gate_up, adapter_in, parts, cols, wide):
    hidden = gate_up.shape[3]
    rank_cols = adapter_in.shape[2]
    pieces = 1
    return pl.pallas_call(
        prepare_kernel,
        out_shape=jax.ShapeDtypeStruct((parts, wide, 2 * hidden + rank_cols), BF16),
        grid_spec=pltpu.PrefetchScalarGridSpec(
            num_scalar_prefetch=1,
            grid=(parts,),
            in_specs=[
                pl.BlockSpec((1, cols, 2, hidden), lambda s, order: (0, order[s], 0, 0)),
                pl.BlockSpec((1, cols, rank_cols), lambda s, order: (0, order[s], 0)),
            ],
            out_specs=pl.BlockSpec((1, wide, 2 * hidden + rank_cols), lambda s, order: (s, 0, 0)),
        ),
        compiler_params=params(),
        cost_estimate=cost(0, 11_000_000),
    )(order, gate_up, adapter_in)


def expert_kernel(cols, width, x0, x1, x2, top, low, into_ref, up_ref, out_ref, mapped_ref):
    hidden = out_ref.shape[1]
    step = pl.program_id(0)
    half = top.shape[0]

    @pl.when(step == 0)
    def _():
        mapped_ref[...] = jnp.dot(x0[...], into_ref[0], preferred_element_type=F32)

    for s, x in ((1, x1), (2, x2)):

        @pl.when(step == s)
        def _():
            mapped_ref[...] += jnp.dot(x[...], into_ref[0], preferred_element_type=F32)

    @pl.when(step == 3)
    def _():
        mapped_ref[:half] += jnp.dot(top[...], into_ref[0], preferred_element_type=F32)
        mapped_ref[half:] += jnp.dot(low[...], into_ref[0], preferred_element_type=F32)

        def norm_part(x):
            return x[:, cols + 1 : cols + 2].astype(F32) + x[:, cols + 2 : cols + 3].astype(F32)

        square = jnp.concatenate([norm_part(top), norm_part(low)], axis=0)
        square = square + norm_part(x0) + norm_part(x1) + norm_part(x2)
        inverse = lax.rsqrt(square / width + 1e-05)
        tenant = x0[:, cols : cols + 1].astype(F32)
        low_rank = mapped_ref[:, 2 * hidden :] * inverse
        owner = lax.broadcasted_iota(jnp.int32, low_rank.shape, 1) // RANK
        low_rank = jnp.where(owner.astype(F32) == tenant, low_rank, 0.0).astype(BF16)
        extra = jnp.dot(low_rank, up_ref[...], preferred_element_type=F32)
        gate_part = mapped_ref[:, :hidden] * inverse + extra[:, :hidden]
        up_part = mapped_ref[:, hidden : 2 * hidden] * inverse + extra[:, hidden:]
        active = gate_part * jax.nn.sigmoid(1.702 * gate_part) * (up_part + 1.0)
        out_ref[...] = active.astype(BF16)


def expert_hidden(blocks, into, up_map, cols, width):
    rows, wide = blocks[0].shape
    hidden = up_map.shape[1] // 2
    return pl.pallas_call(
        functools.partial(expert_kernel, cols, width),
        out_shape=jax.ShapeDtypeStruct((rows, hidden), BF16),
        grid=(4,),
        in_specs=[whole(block.shape) for block in blocks]
        + [pl.BlockSpec((1,) + into.shape[1:], lambda s: (s, 0, 0)), whole(up_map.shape)],
        out_specs=whole((rows, hidden)),
        scratch_shapes=[pltpu.VMEM((rows, into.shape[2]), F32)],
        compiler_params=params(),
        cost_estimate=cost(2 * rows * 4 * wide * into.shape[2], rows * wide * 8 + into.size * 2),
    )(*blocks, into, up_map)


def down_kernel(h0, h1, h2, top, low, d0, d1, d2, d3, out_ref):
    half = top.shape[0]
    for rows, h3 in ((slice(None, half), top), (slice(half, None), low)):
        total = lax.dot_general(h3[...], d3[...], NT, preferred_element_type=F32)
        for h, d in ((h0, d0), (h1, d1), (h2, d2)):
            total = total + lax.dot_general(h[rows], d[...], NT, preferred_element_type=F32)
        out_ref[rows] = total.astype(BF16)


def expert_down(hidden, down):
    rows, inner = hidden[0].shape
    cols = down[0].shape[0]
    return pl.pallas_call(
        down_kernel,
        out_shape=jax.ShapeDtypeStruct((rows, cols), BF16),
        in_specs=[pl.BlockSpec(memory_space=pltpu.VMEM)] * 9,
        out_specs=pl.BlockSpec(memory_space=pltpu.VMEM),
        compiler_params=params(),
        cost_estimate=cost(2 * rows * 4 * inner * cols, rows * inner * 8 + 4 * inner * cols * 2),
    )(*hidden, *down)


def shards(
    residual_in,
    queries,
    keys_values,
    sink_logits,
    out_proj,
    norm_gain,
    routes,
    route_scores,
    tenants,
    gate_up,
    adapter_in,
    adapter_out,
    down_proj,
):
    tok_rows, cols = residual_in.shape
    width = out_proj.shape[1]
    parts = width // cols
    sources = lax.axis_size("ex")
    hidden_here = gate_up.shape[3]
    rank_cols = adapter_in.shape[2]
    me = lax.axis_index("tp")
    wide = -(-(cols + 3) // LANES) * LANES
    order = jnp.stack([me, (me + 3) % parts, (me + 1) % parts, (me + 2) % parts])

    proj = out_proj.T.reshape(parts, cols, out_proj.shape[0])
    terms = attend(queries, keys_values, sink_logits, proj, parts, cols)
    pick = lambda table, at: lax.dynamic_index_in_dim(table, at % parts, 0, keepdims=False)

    experts = jnp.arange(sources, dtype=jnp.int32)
    named = routes.T[:, None, :] == experts[None, :, None]
    member = jnp.any(named, axis=0)
    score_of = jnp.sum(jnp.where(named, route_scores.T[:, None, :], 0), axis=0).astype(F32)
    steps = jnp.arange(tok_rows, dtype=jnp.int32)
    earlier = (steps[:, None] < steps[None, :]).astype(BF16)
    place = jnp.dot(member.astype(BF16), earlier, preferred_element_type=F32).astype(jnp.int32)
    place = jnp.where(member, place, -1)
    score_sum = jnp.sum(route_scores.astype(F32), axis=1, keepdims=True)
    selects, takes, first = [], [], 0
    for slots in CHUNKS:
        here = first + jnp.arange(slots, dtype=jnp.int32)
        first += slots
        hit = place[:, None, :] == here[None, :, None]
        selects.append(hit.astype(BF16).reshape(sources * slots, tok_rows))
        take = jnp.where(hit, score_of[:, None, :], 0.0).astype(BF16)
        takes.append(take.reshape(sources * slots, tok_rows))

    gain_here = lax.dynamic_slice_in_dim(norm_gain, me * cols, cols)[None, :]
    up_map = adapter_out[0].reshape(rank_cols, 2 * hidden_here)
    blocks = down_proj[0].T.reshape(parts, cols, hidden_here)
    shares = [
        pick(terms, me),
        rotate(pick(terms, me + 1), "tp", 1),
        rotate(pick(terms, me + 3), "tp", -1),
        rotate(pick(terms, me + 2), "tp", 2),
    ]
    terms, blocks = together(terms, blocks)
    slabs = [pick(blocks, me), pick(blocks, me + 1), pick(blocks, me + 3), pick(blocks, me + 2)]
    shares, slabs, selects = together(shares, slabs, selects)
    residual_out, message, sent0 = pl.pallas_call(
        functools.partial(send_kernel, cols),
        out_shape=[
            jax.ShapeDtypeStruct((tok_rows, cols), BF16),
            jax.ShapeDtypeStruct((tok_rows, wide), BF16),
            jax.ShapeDtypeStruct((sources * CHUNKS[0], wide), BF16),
        ],
        compiler_params=params(),
        cost_estimate=cost(200_000_000, 4_000_000),
    )(residual_in, *shares, gain_here, tenants.astype(F32)[:, None], selects[0])
    sent0, slabs, order, message = together(sent0, slabs, order, message)
    into = prepare(order, gate_up, adapter_in, parts, cols, wide)
    down = [slabs[0]] + [rotate(slab, "tp", by) for slab, by in zip(slabs[1:], (1, -1, 2))]

    def dispatch(at, rows):
        rows = rows.reshape(sources, CHUNKS[at], wide)
        got = lax.all_to_all(rows, "ex", split_axis=0, concat_axis=0, tiled=True)
        return got.reshape(sources * CHUNKS[at], wide)

    def give_back(at, out):
        out = out.reshape(sources, CHUNKS[at], cols)
        back = lax.all_to_all(out, "ex", split_axis=0, concat_axis=0, tiled=True)
        return back.reshape(sources * CHUNKS[at], cols)

    def hidden(blocks):
        return expert_hidden(blocks, into, up_map, cols, width)

    got0 = dispatch(0, sent0)
    got0, message, down, into = together(got0, message, down, into)
    got1 = dispatch(1, gather_rows(selects[1], message))
    active0 = hidden(ring_gather(got0))
    got1, active0, message = together(got1, active0, message)
    got2 = dispatch(2, gather_rows(selects[2], message))
    active0 = ring_gather(active0)
    active1 = hidden(ring_gather(got1))
    got2, active0, active1 = together(got2, active0, active1)
    back0 = give_back(0, expert_down(active0, down))
    active1 = ring_gather(active1)
    active2 = hidden(ring_gather(got2))
    back0, active1, active2 = together(back0, active1, active2)
    back1 = give_back(1, expert_down(active1, down))
    active2 = ring_gather(active2)
    back1, active2 = together(back1, active2)
    back2 = give_back(2, expert_down(active2, down))
    mixed = jnp.zeros((tok_rows, cols), F32)
    for take, back in zip(takes, (back0, back1, back2)):
        mixed = mixed + lax.dot_general(
            take, back, (((0,), (0,)), ((), ())), preferred_element_type=F32
        )
    expert_mix = (mixed / score_sum).astype(BF16)
    return (residual_out, expert_mix)


def solution(mesh):
    in_specs = (
        P("ex", "tp"),
        P("ex", "tp"),
        P("ex", "tp", None),
        P("tp"),
        P("tp", None),
        P(),
        P("ex", None),
        P("ex", None),
        P("ex"),
        P("ex", None, None, "tp"),
        P("ex", None, None),
        P("ex", None, None, "tp"),
        P("ex", "tp", None),
    )
    out_specs = (P("ex", "tp"), P("ex", "tp"))
    return jax.shard_map(shards, mesh=mesh, in_specs=in_specs, out_specs=out_specs, check_vma=False)
```

```python
import functools

import jax
import jax.numpy as jnp
from jax import lax
from jax.experimental import pallas as pl
from jax.experimental.pallas import tpu as pltpu
from jax.sharding import PartitionSpec as P

WINDOW = 128
TOP = 4
RANK = 16
LANES = 128
CHUNKS = (8, 8, 4)
VMEM_LIMIT = 48 * 1024 * 1024
BF16, F32 = jnp.bfloat16, jnp.float32
NT = (((1,), (1,)), ((), ()))


def params():
    return pltpu.CompilerParams(vmem_limit_bytes=VMEM_LIMIT)


def whole(shape):
    return pl.BlockSpec(shape, lambda *_: (0,) * len(shape))


def cost(flops, moved):
    return pl.CostEstimate(flops=flops, bytes_accessed=moved, transcendentals=0)


def together(*values):
    return lax.optimization_barrier(values)


def from_behind(value, axis, steps):
    count = lax.axis_size(axis)
    initial, last = (max(0, -steps), min(count, count - steps))
    return lax.ppermute(value, axis, [(source, source + steps) for source in range(initial, last)])


def rotate(value, axis, steps):
    count = lax.axis_size(axis)
    return lax.ppermute(value, axis, [(source, (source + steps) % count) for source in range(count)])


def ring_gather(value):
    half = value.shape[0] // 2
    behind = rotate(value, "tp", 1)
    ahead = rotate(value, "tp", -1)
    return value, behind, ahead, rotate(behind[:half], "tp", 1), rotate(ahead[half:], "tp", -1)


def attend_kernel(heads, head_size, first_ref, q_ref, before_ref, kv_ref, sink_ref, proj_ref, out_ref):
    rows = q_ref.shape[0]
    rim = before_ref.shape[0]
    near = jnp.concatenate([before_ref[...], kv_ref[...]], axis=0)
    keys_only = near[:, :head_size]
    values_only = near[:, head_size:]
    at = lax.broadcasted_iota(jnp.int32, (rows, rim + rows), 0)
    key_at = lax.broadcasted_iota(jnp.int32, (rows, rim + rows), 1)
    distance = at + rim - key_at
    allowed = (distance >= 0) & (distance < WINDOW) & (key_at + first_ref[0] >= rim)
    pieces = []
    for head in range(heads):
        query = q_ref[:, head * head_size : (head + 1) * head_size]
        scores = lax.dot_general(query, keys_only, NT, preferred_element_type=F32)
        scores = scores * head_size ** (-0.5)
        numerators = jnp.where(allowed, jnp.exp(scores), 0.0)
        total = jnp.exp(sink_ref[:, head : head + 1]) + jnp.sum(numerators, axis=1, keepdims=True)
        weights = (numerators / total).astype(BF16)
        pieces.append(jnp.dot(weights, values_only, preferred_element_type=F32).astype(BF16))
    attended = jnp.concatenate(pieces, axis=1)
    for part in range(out_ref.shape[0]):
        out_ref[part] = lax.dot_general(
            attended, proj_ref[part], NT, preferred_element_type=F32
        ).astype(BF16)


def attend(queries, keys_values, sink_logits, proj, parts, cols):
    rows = queries.shape[0]
    heads = sink_logits.shape[0]
    head_size = keys_values.shape[2] // 2
    own = keys_values.reshape(rows, 2 * head_size)
    before = from_behind(own[rows - WINDOW :], "ex", 1)
    first = (lax.axis_index("ex") * rows).reshape(1)
    return pl.pallas_call(
        functools.partial(attend_kernel, heads, head_size),
        out_shape=jax.ShapeDtypeStruct((parts, rows, cols), BF16),
        in_specs=[pl.BlockSpec(memory_space=pltpu.SMEM)]
        + [pl.BlockSpec(memory_space=pltpu.VMEM)] * 5,
        out_specs=pl.BlockSpec(memory_space=pltpu.VMEM),
        compiler_params=params(),
        cost_estimate=cost(700_000_000, 5_000_000),
    )(first, queries, before, own, sink_logits.reshape(1, heads), proj)


def send_kernel(
    cols, res_ref, t0, t1, t2, t3, gain_ref, tenant_ref, select_ref, out_ref, message_ref, sent_ref
):
    share = t0[...].astype(F32) + t1[...].astype(F32) + t2[...].astype(F32) + t3[...].astype(F32)
    residual = (res_ref[...].astype(F32) + share).astype(BF16)
    out_ref[...] = residual
    rows = residual.astype(F32)
    squares = jnp.sum(rows * rows, axis=1, keepdims=True)
    top = squares.astype(BF16).astype(F32)
    low = squares - top
    wide = message_ref.shape[1]
    lane = lax.broadcasted_iota(jnp.int32, (rows.shape[0], wide - cols), 1)
    extra = jnp.where(
        lane == 0, tenant_ref[...], jnp.where(lane == 1, top, jnp.where(lane == 2, low, 0.0))
    )
    message = jnp.concatenate([rows * gain_ref[...], extra], axis=1).astype(BF16)
    message_ref[...] = message
    sent_ref[...] = jnp.dot(select_ref[...], message, preferred_element_type=F32).astype(BF16)


def gather_kernel(select_ref, message_ref, sent_ref):
    sent_ref[...] = jnp.dot(
        select_ref[...], message_ref[...], preferred_element_type=F32
    ).astype(BF16)


def gather_rows(select, message):
    return pl.pallas_call(
        gather_kernel,
        out_shape=jax.ShapeDtypeStruct((select.shape[0], message.shape[1]), BF16),
        compiler_params=params(),
        cost_estimate=cost(2 * select.size * message.shape[1], 2_000_000),
    )(select, message)


def prepare_kernel(order_ref, gate_up_ref, in_ref, out_ref):
    cols = in_ref.shape[1]
    hidden = gate_up_ref.shape[3]
    both = gate_up_ref[0].astype(F32)
    out_ref[0, :cols, :hidden] = both[:, 0, :].astype(BF16)
    out_ref[0, :cols, hidden : 2 * hidden] = both[:, 1, :].astype(BF16)
    out_ref[0, :cols, 2 * hidden :] = in_ref[0]
    out_ref[0, cols:, :] = jnp.zeros_like(out_ref[0, cols:, :])


def prepare(order, gate_up, adapter_in, parts, cols, wide):
    hidden = gate_up.shape[3]
    rank_cols = adapter_in.shape[2]
    pieces = 1
    return pl.pallas_call(
        prepare_kernel,
        out_shape=jax.ShapeDtypeStruct((parts, wide, 2 * hidden + rank_cols), BF16),
        grid_spec=pltpu.PrefetchScalarGridSpec(
            num_scalar_prefetch=1,
            grid=(parts,),
            in_specs=[
                pl.BlockSpec((1, cols, 2, hidden), lambda s, order: (0, order[s], 0, 0)),
                pl.BlockSpec((1, cols, rank_cols), lambda s, order: (0, order[s], 0)),
            ],
            out_specs=pl.BlockSpec((1, wide, 2 * hidden + rank_cols), lambda s, order: (s, 0, 0)),
        ),
        compiler_params=params(),
        cost_estimate=cost(0, 11_000_000),
    )(order, gate_up, adapter_in)


def expert_kernel(cols, width, x0, x1, x2, top, low, into_ref, up_ref, out_ref, mapped_ref):
    hidden = out_ref.shape[1]
    step = pl.program_id(0)
    half = top.shape[0]

    @pl.when(step == 0)
    def _():
        mapped_ref[...] = jnp.dot(x0[...], into_ref[0], preferred_element_type=F32)

    for s, x in ((1, x1), (2, x2)):

        @pl.when(step == s)
        def _():
            mapped_ref[...] += jnp.dot(x[...], into_ref[0], preferred_element_type=F32)

    @pl.when(step == 3)
    def _():
        mapped_ref[:half] += jnp.dot(top[...], into_ref[0], preferred_element_type=F32)
        mapped_ref[half:] += jnp.dot(low[...], into_ref[0], preferred_element_type=F32)

        def norm_part(x):
            return x[:, cols + 1 : cols + 2].astype(F32) + x[:, cols + 2 : cols + 3].astype(F32)

        square = jnp.concatenate([norm_part(top), norm_part(low)], axis=0)
        square = square + norm_part(x0) + norm_part(x1) + norm_part(x2)
        inverse = lax.rsqrt(square / width + 1e-05)
        tenant = x0[:, cols : cols + 1].astype(F32)
        low_rank = mapped_ref[:, 2 * hidden :] * inverse
        owner = lax.broadcasted_iota(jnp.int32, low_rank.shape, 1) // RANK
        low_rank = jnp.where(owner.astype(F32) == tenant, low_rank, 0.0).astype(BF16)
        extra = jnp.dot(low_rank, up_ref[...], preferred_element_type=F32)
        gate_part = mapped_ref[:, :hidden] * inverse + extra[:, :hidden]
        up_part = mapped_ref[:, hidden : 2 * hidden] * inverse + extra[:, hidden:]
        active = gate_part * jax.nn.sigmoid(1.702 * gate_part) * (up_part + 1.0)
        out_ref[...] = active.astype(BF16)


def expert_hidden(blocks, into, up_map, cols, width):
    rows, wide = blocks[0].shape
    hidden = up_map.shape[1] // 2
    return pl.pallas_call(
        functools.partial(expert_kernel, cols, width),
        out_shape=jax.ShapeDtypeStruct((rows, hidden), BF16),
        grid=(4,),
        in_specs=[whole(block.shape) for block in blocks]
        + [pl.BlockSpec((1,) + into.shape[1:], lambda s: (s, 0, 0)), whole(up_map.shape)],
        out_specs=whole((rows, hidden)),
        scratch_shapes=[pltpu.VMEM((rows, into.shape[2]), F32)],
        compiler_params=params(),
        cost_estimate=cost(12000000000, 1000000),
    )(*blocks, into, up_map)


def down_kernel(h0, h1, h2, top, low, d0, d1, d2, d3, out_ref):
    half = top.shape[0]
    for rows, h3 in ((slice(None, half), top), (slice(half, None), low)):
        total = lax.dot_general(h3[...], d3[...], NT, preferred_element_type=F32)
        for h, d in ((h0, d0), (h1, d1), (h2, d2)):
            total = total + lax.dot_general(h[rows], d[...], NT, preferred_element_type=F32)
        out_ref[rows] = total.astype(BF16)


def expert_down(hidden, down):
    rows, inner = hidden[0].shape
    cols = down[0].shape[0]
    return pl.pallas_call(
        down_kernel,
        out_shape=jax.ShapeDtypeStruct((rows, cols), BF16),
        in_specs=[pl.BlockSpec(memory_space=pltpu.VMEM)] * 9,
        out_specs=pl.BlockSpec(memory_space=pltpu.VMEM),
        compiler_params=params(),
        cost_estimate=cost(2 * rows * 4 * inner * cols, rows * inner * 8 + 4 * inner * cols * 2),
    )(*hidden, *down)


def shards(
    residual_in,
    queries,
    keys_values,
    sink_logits,
    out_proj,
    norm_gain,
    routes,
    route_scores,
    tenants,
    gate_up,
    adapter_in,
    adapter_out,
    down_proj,
):
    tok_rows, cols = residual_in.shape
    width = out_proj.shape[1]
    parts = width // cols
    sources = lax.axis_size("ex")
    hidden_here = gate_up.shape[3]
    rank_cols = adapter_in.shape[2]
    me = lax.axis_index("tp")
    wide = -(-(cols + 3) // LANES) * LANES
    order = jnp.stack([me, (me + 3) % parts, (me + 1) % parts, (me + 2) % parts])

    proj = out_proj.T.reshape(parts, cols, out_proj.shape[0])
    terms = attend(queries, keys_values, sink_logits, proj, parts, cols)
    pick = lambda table, at: lax.dynamic_index_in_dim(table, at % parts, 0, keepdims=False)

    experts = jnp.arange(sources, dtype=jnp.int32)
    named = routes.T[:, None, :] == experts[None, :, None]
    member = jnp.any(named, axis=0)
    score_of = jnp.sum(jnp.where(named, route_scores.T[:, None, :], 0), axis=0).astype(F32)
    steps = jnp.arange(tok_rows, dtype=jnp.int32)
    earlier = (steps[:, None] < steps[None, :]).astype(BF16)
    place = jnp.dot(member.astype(BF16), earlier, preferred_element_type=F32).astype(jnp.int32)
    place = jnp.where(member, place, -1)
    score_sum = jnp.sum(route_scores.astype(F32), axis=1, keepdims=True)
    selects, takes, first = [], [], 0
    for slots in CHUNKS:
        here = first + jnp.arange(slots, dtype=jnp.int32)
        first += slots
        hit = place[:, None, :] == here[None, :, None]
        selects.append(hit.astype(BF16).reshape(sources * slots, tok_rows))
        take = jnp.where(hit, score_of[:, None, :], 0.0).astype(BF16)
        takes.append(take.reshape(sources * slots, tok_rows))

    gain_here = lax.dynamic_slice_in_dim(norm_gain, me * cols, cols)[None, :]
    up_map = adapter_out[0].reshape(rank_cols, 2 * hidden_here)
    blocks = down_proj[0].T.reshape(parts, cols, hidden_here)
    shares = [
        pick(terms, me),
        rotate(pick(terms, me + 1), "tp", 1),
        rotate(pick(terms, me + 3), "tp", -1),
        rotate(pick(terms, me + 2), "tp", 2),
    ]
    terms, blocks = together(terms, blocks)
    slabs = [pick(blocks, me), pick(blocks, me + 1), pick(blocks, me + 3), pick(blocks, me + 2)]
    shares, slabs, selects = together(shares, slabs, selects)
    residual_out, message, sent0 = pl.pallas_call(
        functools.partial(send_kernel, cols),
        out_shape=[
            jax.ShapeDtypeStruct((tok_rows, cols), BF16),
            jax.ShapeDtypeStruct((tok_rows, wide), BF16),
            jax.ShapeDtypeStruct((sources * CHUNKS[0], wide), BF16),
        ],
        compiler_params=params(),
        cost_estimate=cost(200_000_000, 4_000_000),
    )(residual_in, *shares, gain_here, tenants.astype(F32)[:, None], selects[0])
    sent0, slabs, order, message = together(sent0, slabs, order, message)
    into = prepare(order, gate_up, adapter_in, parts, cols, wide)
    down = [slabs[0]] + [rotate(slab, "tp", by) for slab, by in zip(slabs[1:], (1, -1, 2))]

    def dispatch(at, rows):
        rows = rows.reshape(sources, CHUNKS[at], wide)
        got = lax.all_to_all(rows, "ex", split_axis=0, concat_axis=0, tiled=True)
        return got.reshape(sources * CHUNKS[at], wide)

    def give_back(at, out):
        out = out.reshape(sources, CHUNKS[at], cols)
        back = lax.all_to_all(out, "ex", split_axis=0, concat_axis=0, tiled=True)
        return back.reshape(sources * CHUNKS[at], cols)

    def hidden(blocks):
        return expert_hidden(blocks, into, up_map, cols, width)

    got0 = dispatch(0, sent0)
    got0, message, down, into = together(got0, message, down, into)
    got1 = dispatch(1, gather_rows(selects[1], message))
    active0 = hidden(ring_gather(got0))
    got1, active0, message = together(got1, active0, message)
    got2 = dispatch(2, gather_rows(selects[2], message))
    active0 = ring_gather(active0)
    active1 = hidden(ring_gather(got1))
    got2, active0, active1 = together(got2, active0, active1)
    back0 = give_back(0, expert_down(active0, down))
    active1 = ring_gather(active1)
    active2 = hidden(ring_gather(got2))
    back0, active1, active2 = together(back0, active1, active2)
    back1 = give_back(1, expert_down(active1, down))
    active2 = ring_gather(active2)
    back1, active2 = together(back1, active2)
    back2 = give_back(2, expert_down(active2, down))
    mixed = jnp.zeros((tok_rows, cols), F32)
    for take, back in zip(takes, (back0, back1, back2)):
        mixed = mixed + lax.dot_general(
            take, back, (((0,), (0,)), ((), ())), preferred_element_type=F32
        )
    expert_mix = (mixed / score_sum).astype(BF16)
    return (residual_out, expert_mix)


def solution(mesh):
    in_specs = (
        P("ex", "tp"),
        P("ex", "tp"),
        P("ex", "tp", None),
        P("tp"),
        P("tp", None),
        P(),
        P("ex", None),
        P("ex", None),
        P("ex"),
        P("ex", None, None, "tp"),
        P("ex", None, None),
        P("ex", None, None, "tp"),
        P("ex", "tp", None),
    )
    out_specs = (P("ex", "tp"), P("ex", "tp"))
    return jax.shard_map(shards, mesh=mesh, in_specs=in_specs, out_specs=out_specs, check_vma=False)
```

```python
import functools

import jax
import jax.numpy as jnp
from jax import lax
from jax.experimental import pallas as pl
from jax.experimental.pallas import tpu as pltpu
from jax.sharding import PartitionSpec as P

WINDOW = 128
TOP = 4
RANK = 16
LANES = 128
CHUNKS = (8, 8, 4)
VMEM_LIMIT = 48 * 1024 * 1024
BF16, F32 = jnp.bfloat16, jnp.float32
NT = (((1,), (1,)), ((), ()))


def params():
    return pltpu.CompilerParams(vmem_limit_bytes=VMEM_LIMIT)


def whole(shape):
    return pl.BlockSpec(shape, lambda *_: (0,) * len(shape))


def cost(flops, moved):
    return pl.CostEstimate(flops=flops, bytes_accessed=moved, transcendentals=0)


def together(*values):
    return lax.optimization_barrier(values)


def from_behind(value, axis, steps):
    count = lax.axis_size(axis)
    initial, last = (max(0, -steps), min(count, count - steps))
    return lax.ppermute(value, axis, [(source, source + steps) for source in range(initial, last)])


def rotate(value, axis, steps):
    count = lax.axis_size(axis)
    return lax.ppermute(value, axis, [(source, (source + steps) % count) for source in range(count)])


def ring_gather(value):
    half = value.shape[0] // 2
    behind = rotate(value, "tp", 1)
    ahead = rotate(value, "tp", -1)
    return value, behind, ahead, rotate(behind[:half], "tp", 1), rotate(ahead[half:], "tp", -1)


def attend_kernel(heads, head_size, first_ref, q_ref, before_ref, kv_ref, sink_ref, proj_ref, out_ref):
    rows = q_ref.shape[0]
    rim = before_ref.shape[0]
    near = jnp.concatenate([before_ref[...], kv_ref[...]], axis=0)
    keys_only = near[:, :head_size]
    values_only = near[:, head_size:]
    at = lax.broadcasted_iota(jnp.int32, (rows, rim + rows), 0)
    key_at = lax.broadcasted_iota(jnp.int32, (rows, rim + rows), 1)
    distance = at + rim - key_at
    allowed = (distance >= 0) & (distance < WINDOW) & (key_at + first_ref[0] >= rim)
    pieces = []
    for head in range(heads):
        query = q_ref[:, head * head_size : (head + 1) * head_size]
        scores = lax.dot_general(query, keys_only, NT, preferred_element_type=F32)
        scores = scores * head_size ** (-0.5)
        numerators = jnp.where(allowed, jnp.exp(scores), 0.0)
        total = jnp.exp(sink_ref[:, head : head + 1]) + jnp.sum(numerators, axis=1, keepdims=True)
        weights = (numerators / total).astype(BF16)
        pieces.append(jnp.dot(weights, values_only, preferred_element_type=F32).astype(BF16))
    attended = jnp.concatenate(pieces, axis=1)
    for part in range(out_ref.shape[0]):
        out_ref[part] = lax.dot_general(
            attended, proj_ref[part], NT, preferred_element_type=F32
        ).astype(BF16)


def attend(queries, keys_values, sink_logits, proj, parts, cols):
    rows = queries.shape[0]
    heads = sink_logits.shape[0]
    head_size = keys_values.shape[2] // 2
    own = keys_values.reshape(rows, 2 * head_size)
    before = from_behind(own[rows - WINDOW :], "ex", 1)
    first = (lax.axis_index("ex") * rows).reshape(1)
    return pl.pallas_call(
        functools.partial(attend_kernel, heads, head_size),
        out_shape=jax.ShapeDtypeStruct((parts, rows, cols), BF16),
        in_specs=[pl.BlockSpec(memory_space=pltpu.SMEM)]
        + [pl.BlockSpec(memory_space=pltpu.VMEM)] * 5,
        out_specs=pl.BlockSpec(memory_space=pltpu.VMEM),
        compiler_params=params(),
        cost_estimate=cost(700_000_000, 5_000_000),
    )(first, queries, before, own, sink_logits.reshape(1, heads), proj)


def send_kernel(
    cols, res_ref, t0, t1, t2, t3, gain_ref, tenant_ref, select_ref, out_ref, message_ref, sent_ref
):
    share = t0[...].astype(F32) + t1[...].astype(F32) + t2[...].astype(F32) + t3[...].astype(F32)
    residual = (res_ref[...].astype(F32) + share).astype(BF16)
    out_ref[...] = residual
    rows = residual.astype(F32)
    squares = jnp.sum(rows * rows, axis=1, keepdims=True)
    top = squares.astype(BF16).astype(F32)
    low = squares - top
    wide = message_ref.shape[1]
    lane = lax.broadcasted_iota(jnp.int32, (rows.shape[0], wide - cols), 1)
    extra = jnp.where(
        lane == 0, tenant_ref[...], jnp.where(lane == 1, top, jnp.where(lane == 2, low, 0.0))
    )
    message = jnp.concatenate([rows * gain_ref[...], extra], axis=1).astype(BF16)
    message_ref[...] = message
    sent_ref[...] = jnp.dot(select_ref[...], message, preferred_element_type=F32).astype(BF16)


def gather_kernel(select_ref, message_ref, sent_ref):
    sent_ref[...] = jnp.dot(
        select_ref[...], message_ref[...], preferred_element_type=F32
    ).astype(BF16)


def gather_rows(select, message):
    return pl.pallas_call(
        gather_kernel,
        out_shape=jax.ShapeDtypeStruct((select.shape[0], message.shape[1]), BF16),
        compiler_params=params(),
        cost_estimate=cost(2 * select.size * message.shape[1], 2_000_000),
    )(select, message)


def prepare_kernel(order_ref, gate_up_ref, in_ref, out_ref):
    cols = in_ref.shape[1]
    hidden = gate_up_ref.shape[3]
    both = gate_up_ref[0].astype(F32)
    out_ref[0, :cols, :hidden] = both[:, 0, :].astype(BF16)
    out_ref[0, :cols, hidden : 2 * hidden] = both[:, 1, :].astype(BF16)
    out_ref[0, :cols, 2 * hidden :] = in_ref[0]
    out_ref[0, cols:, :] = jnp.zeros_like(out_ref[0, cols:, :])


def prepare(order, gate_up, adapter_in, parts, cols, wide):
    hidden = gate_up.shape[3]
    rank_cols = adapter_in.shape[2]
    pieces = 1
    return pl.pallas_call(
        prepare_kernel,
        out_shape=jax.ShapeDtypeStruct((parts, wide, 2 * hidden + rank_cols), BF16),
        grid_spec=pltpu.PrefetchScalarGridSpec(
            num_scalar_prefetch=1,
            grid=(parts,),
            in_specs=[
                pl.BlockSpec((1, cols, 2, hidden), lambda s, order: (0, order[s], 0, 0)),
                pl.BlockSpec((1, cols, rank_cols), lambda s, order: (0, order[s], 0)),
            ],
            out_specs=pl.BlockSpec((1, wide, 2 * hidden + rank_cols), lambda s, order: (s, 0, 0)),
        ),
        compiler_params=params(),
        cost_estimate=cost(0, 11_000_000),
    )(order, gate_up, adapter_in)


def expert_kernel(cols, width, x0, x1, x2, top, low, into_ref, up_ref, out_ref, mapped_ref):
    hidden = out_ref.shape[1]
    step = pl.program_id(0)
    half = top.shape[0]

    @pl.when(step == 0)
    def _():
        mapped_ref[...] = jnp.dot(x0[...], into_ref[0], preferred_element_type=F32)

    for s, x in ((1, x1), (2, x2)):

        @pl.when(step == s)
        def _():
            mapped_ref[...] += jnp.dot(x[...], into_ref[0], preferred_element_type=F32)

    @pl.when(step == 3)
    def _():
        mapped_ref[:half] += jnp.dot(top[...], into_ref[0], preferred_element_type=F32)
        mapped_ref[half:] += jnp.dot(low[...], into_ref[0], preferred_element_type=F32)

        def norm_part(x):
            return x[:, cols + 1 : cols + 2].astype(F32) + x[:, cols + 2 : cols + 3].astype(F32)

        square = jnp.concatenate([norm_part(top), norm_part(low)], axis=0)
        square = square + norm_part(x0) + norm_part(x1) + norm_part(x2)
        inverse = lax.rsqrt(square / width + 1e-05)
        tenant = x0[:, cols : cols + 1].astype(F32)
        low_rank = mapped_ref[:, 2 * hidden :] * inverse
        owner = lax.broadcasted_iota(jnp.int32, low_rank.shape, 1) // RANK
        low_rank = jnp.where(owner.astype(F32) == tenant, low_rank, 0.0).astype(BF16)
        extra = jnp.dot(low_rank, up_ref[...], preferred_element_type=F32)
        gate_part = mapped_ref[:, :hidden] * inverse + extra[:, :hidden]
        up_part = mapped_ref[:, hidden : 2 * hidden] * inverse + extra[:, hidden:]
        active = gate_part * jax.nn.sigmoid(1.702 * gate_part) * (up_part + 1.0)
        out_ref[...] = active.astype(BF16)


def expert_hidden(blocks, into, up_map, cols, width):
    rows, wide = blocks[0].shape
    hidden = up_map.shape[1] // 2
    return pl.pallas_call(
        functools.partial(expert_kernel, cols, width),
        out_shape=jax.ShapeDtypeStruct((rows, hidden), BF16),
        grid=(4,),
        in_specs=[whole(block.shape) for block in blocks]
        + [pl.BlockSpec((1,) + into.shape[1:], lambda s: (s, 0, 0)), whole(up_map.shape)],
        out_specs=whole((rows, hidden)),
        scratch_shapes=[pltpu.VMEM((rows, into.shape[2]), F32)],
        compiler_params=params(),
        cost_estimate=cost(12000000000, 1000000),
    )(*blocks, into, up_map)


def down_kernel(h0, h1, h2, top, low, d0, d1, d2, d3, out_ref):
    half = top.shape[0]
    for rows, h3 in ((slice(None, half), top), (slice(half, None), low)):
        total = lax.dot_general(h3[...], d3[...], NT, preferred_element_type=F32)
        for h, d in ((h0, d0), (h1, d1), (h2, d2)):
            total = total + lax.dot_general(h[rows], d[...], NT, preferred_element_type=F32)
        out_ref[rows] = total.astype(BF16)


def expert_down(hidden, down):
    rows, inner = hidden[0].shape
    cols = down[0].shape[0]
    return pl.pallas_call(
        down_kernel,
        out_shape=jax.ShapeDtypeStruct((rows, cols), BF16),
        in_specs=[pl.BlockSpec(memory_space=pltpu.VMEM)] * 9,
        out_specs=pl.BlockSpec(memory_space=pltpu.VMEM),
        compiler_params=params(),
        cost_estimate=cost(2 * rows * 4 * inner * cols, rows * inner * 8 + 4 * inner * cols * 2),
    )(*hidden, *down)


def shards(
    residual_in,
    queries,
    keys_values,
    sink_logits,
    out_proj,
    norm_gain,
    routes,
    route_scores,
    tenants,
    gate_up,
    adapter_in,
    adapter_out,
    down_proj,
):
    tok_rows, cols = residual_in.shape
    width = out_proj.shape[1]
    parts = width // cols
    sources = lax.axis_size("ex")
    hidden_here = gate_up.shape[3]
    rank_cols = adapter_in.shape[2]
    me = lax.axis_index("tp")
    wide = -(-(cols + 3) // LANES) * LANES
    order = jnp.stack([me, (me + 3) % parts, (me + 1) % parts, (me + 2) % parts])

    proj = out_proj.T.reshape(parts, cols, out_proj.shape[0])
    terms = attend(queries, keys_values, sink_logits, proj, parts, cols)
    pick = lambda table, at: lax.dynamic_index_in_dim(table, at % parts, 0, keepdims=False)

    experts = jnp.arange(sources, dtype=jnp.int32)
    named = routes.T[:, None, :] == experts[None, :, None]
    member = jnp.any(named, axis=0)
    score_of = jnp.sum(jnp.where(named, route_scores.T[:, None, :], 0), axis=0).astype(F32)
    steps = jnp.arange(tok_rows, dtype=jnp.int32)
    earlier = (steps[:, None] < steps[None, :]).astype(BF16)
    place = jnp.dot(member.astype(BF16), earlier, preferred_element_type=F32).astype(jnp.int32)
    place = jnp.where(member, place, -1)
    score_sum = jnp.sum(route_scores.astype(F32), axis=1, keepdims=True)
    selects, takes, first = [], [], 0
    for slots in CHUNKS:
        here = first + jnp.arange(slots, dtype=jnp.int32)
        first += slots
        hit = place[:, None, :] == here[None, :, None]
        selects.append(hit.astype(BF16).reshape(sources * slots, tok_rows))
        take = jnp.where(hit, score_of[:, None, :], 0.0).astype(BF16)
        takes.append(take.reshape(sources * slots, tok_rows))

    gain_here = lax.dynamic_slice_in_dim(norm_gain, me * cols, cols)[None, :]
    up_map = adapter_out[0].reshape(rank_cols, 2 * hidden_here)
    blocks = down_proj[0].T.reshape(parts, cols, hidden_here)
    shares = [
        pick(terms, me),
        rotate(pick(terms, me + 1), "tp", 1),
        rotate(pick(terms, me + 3), "tp", -1),
        rotate(pick(terms, me + 2), "tp", 2),
    ]
    terms, blocks = together(terms, blocks)
    slabs = [pick(blocks, me), pick(blocks, me + 1), pick(blocks, me + 3), pick(blocks, me + 2)]
    shares, slabs, selects = together(shares, slabs, selects)
    residual_out, message, sent0 = pl.pallas_call(
        functools.partial(send_kernel, cols),
        out_shape=[
            jax.ShapeDtypeStruct((tok_rows, cols), BF16),
            jax.ShapeDtypeStruct((tok_rows, wide), BF16),
            jax.ShapeDtypeStruct((sources * CHUNKS[0], wide), BF16),
        ],
        compiler_params=params(),
        cost_estimate=cost(200_000_000, 4_000_000),
    )(residual_in, *shares, gain_here, tenants.astype(F32)[:, None], selects[0])
    sent0, slabs, order, message = together(sent0, slabs, order, message)
    into = prepare(order, gate_up, adapter_in, parts, cols, wide)
    down = [slabs[0]] + [rotate(slab, "tp", by) for slab, by in zip(slabs[1:], (1, -1, 2))]

    def dispatch(at, rows):
        rows = rows.reshape(sources, CHUNKS[at], wide)
        got = lax.all_to_all(rows, "ex", split_axis=0, concat_axis=0, tiled=True)
        return got.reshape(sources * CHUNKS[at], wide)

    def give_back(at, out):
        out = out.reshape(sources, CHUNKS[at], cols)
        back = lax.all_to_all(out, "ex", split_axis=0, concat_axis=0, tiled=True)
        return back.reshape(sources * CHUNKS[at], cols)

    def hidden(blocks):
        return expert_hidden(blocks, into, up_map, cols, width)

    got0 = dispatch(0, sent0)
    got0, message, down, into = together(got0, message, down, into)
    got1 = dispatch(1, gather_rows(selects[1], message))
    active0 = hidden(ring_gather(got0))
    got1, active0, message = together(got1, active0, message)
    got2 = dispatch(2, gather_rows(selects[2], message))
    active0 = ring_gather(active0)
    active1 = hidden(ring_gather(got1))
    got2, active0, active1 = together(got2, active0, active1)
    back0 = give_back(0, expert_down(active0, down))
    active1 = ring_gather(active1)
    active2 = hidden(ring_gather(got2))
    back0, active1, active2 = together(back0, active1, active2)
    back1 = give_back(1, expert_down(active1, down))
    out2 = expert_down(ring_gather(active2), down).reshape(sources, CHUNKS[2], cols)
    back1, out2 = together(back1, out2)
    back2 = give_back(2, out2)
    mixed = jnp.zeros((tok_rows, cols), F32)
    for take, back in zip(takes, (back0, back1, back2)):
        mixed = mixed + lax.dot_general(
            take, back, (((0,), (0,)), ((), ())), preferred_element_type=F32
        )
    expert_mix = (mixed / score_sum).astype(BF16)
    return (residual_out, expert_mix)


def solution(mesh):
    in_specs = (
        P("ex", "tp"),
        P("ex", "tp"),
        P("ex", "tp", None),
        P("tp"),
        P("tp", None),
        P(),
        P("ex", None),
        P("ex", None),
        P("ex"),
        P("ex", None, None, "tp"),
        P("ex", None, None),
        P("ex", None, None, "tp"),
        P("ex", "tp", None),
    )
    out_specs = (P("ex", "tp"), P("ex", "tp"))
    return jax.shard_map(shards, mesh=mesh, in_specs=in_specs, out_specs=out_specs, check_vma=False)
```
